128 devices in a mesh: rows: 128 (over z, x, y, core).
Axes of the slice: x: 4, y: 4, z: 4, core: 2. Of those that a mesh axis runs over, the one named last changes fastest.
Arguments:
- matrix_panel: float32 [16, 2097152], P(None, 'rows'), may hold values from -6 to 6
- row_signs: int32 [2097152], P('rows'), may hold values from -1 to 1, as said below
- sample_rows: int32 [4096], replicated, may hold values from 0 to 2097151
Outputs:
- sketch: float32 [16, 4096], P(None, 'rows')
The draws below stay inside these ranges and needn't reach their ends.
Inputs may be any that keep to these rules, and one draw needn't show every extreme that they name: `row_signs`: each entry is -1 or 1.
All inputs are finite; a program needn't handle non-finite values.
Results may differ from the reference program's by a relative error of at most 0.00014.
Values sent between devices are 32-bit elements; how exact they have to be, the bound alone decides.
No kernel may reach another device: no remote copies, remote signals or barrier semaphores. Data moves between devices by JAX's collectives and lax.ppermute only.
A program may use at most 64 MiB of HBM per device.

```python
import math
import jax
import jax.numpy as jnp
from jax import lax

COLS = 16
SAMPLES = 4096
TOTAL_ROWS = 2097152


def draw_row_signs(key, part):
    key = jax.random.fold_in(key, 11)
    return (2 * jax.random.randint(key, (TOTAL_ROWS,), 0, 2) - 1).astype(jnp.int32)


def set_ends(values, stream_key, smallest, top_value):
    longest = values.shape.index(max(values.shape))
    spots = []
    for shift in (0, 1):
        where = [jax.random.randint(jax.random.fold_in(stream_key, axis), (), 0, length) for axis, length in enumerate(values.shape)]
        where[longest] = (where[longest] + shift) % values.shape[longest]
        spots.append(tuple(where))
    return values.at[spots[0]].set(smallest).at[spots[1]].set(top_value)


def level_of(stream_key, dims, cuts, low, high):
    def one(axis_at, shards_of):
        steps = jax.random.uniform(jax.random.fold_in(jax.random.fold_in(stream_key, 6), axis_at), (shards_of,), jnp.float32, low / len(cuts), high / len(cuts))
        return jnp.repeat(jnp.exp(steps), dims[axis_at] // shards_of).reshape((-1,) + (1,) * (len(dims) - axis_at - 1))

    level = one(*cuts[0])
    for cut in cuts[1:]:
        level = level * one(*cut)
    return level


def normal_values(stream_key, extent, scale, most, shards=(), kind=jnp.bfloat16):
    result = scale * jax.random.normal(stream_key, extent, jnp.float32)
    if shards:
        result = result * level_of(stream_key, extent, shards, -0.22, 0.18)
    return jnp.clip(result, -most, most).astype(kind)


def setup_inputs(seed: int = 0) -> dict:
    key_list = jax.random.split(jax.random.key(seed), 4)
    matrix_panel = normal_values(key_list[0], (COLS, TOTAL_ROWS), 1.0, 6.0, ((1, 128),), jnp.float32)
    row_signs = draw_row_signs(jax.random.fold_in(key_list[3], 71), 0)
    sample_rows = set_ends(jax.random.randint(key_list[2], (SAMPLES,), 0, TOTAL_ROWS), jax.random.fold_in(key_list[2], 1), 0, TOTAL_ROWS - 1).astype(jnp.int32)
    return dict(matrix_panel=matrix_panel, row_signs=row_signs, sample_rows=sample_rows)


def hadamard_table(order_size):
    indices = jnp.arange(order_size, dtype=jnp.int32)
    intersection = jnp.bitwise_and(indices[:, None], indices[None, :])
    parity = jnp.zeros((order_size, order_size), jnp.int32)
    for bit_number in range(order_size.bit_length() - 1):
        parity = parity + jnp.bitwise_and(jnp.right_shift(intersection, bit_number), 1)
    return jnp.where(parity % 2 == 0, 1.0, -1.0).astype(jnp.float32)

def local_hadamard(current):
    columns, length = current.shape
    stride = 1
    while stride < length:
        factor_size = min(128, length // stride)
        outer_count = length // (factor_size * stride)
        reshaped = current.reshape(columns, outer_count, factor_size, stride)
        reshaped = jnp.einsum('cofi,gf->cogi', reshaped, hadamard_table(factor_size), precision=lax.Precision.HIGHEST)
        current = reshaped.reshape(columns, length)
        stride = stride * factor_size
    return current

def reference(matrix_panel, row_signs, sample_rows):
    signed = matrix_panel * row_signs.astype(jnp.float32)[None, :]
    transformed = local_hadamard(signed)
    return transformed[:, sample_rows] * (1.0 / math.sqrt(TOTAL_ROWS))
```

```python
import functools
import math

import jax
import jax.numpy as jnp
from jax import lax
from jax.experimental import pallas as pl
from jax.experimental.pallas import tpu as pltpu
from jax.sharding import PartitionSpec as P

LANES = 128
FOLD = 256


def butterflies(parts):
    parts = list(parts)
    half = 1
    while half < len(parts):
        for i in range(len(parts)):
            if not i & half:
                low, high = parts[i], parts[i + half]
                parts[i], parts[i + half] = low + high, low - high
        half *= 2
    return parts


def odd_bits(x, width):
    shift = 1
    while shift < width:
        shift *= 2
    while shift > 1:
        shift //= 2
        x = x ^ (x >> shift)
    return x & 1


def plus_minus(bit):
    return (1 - 2 * bit).astype(jnp.float32)


def sampled_table(rows, position, local_bits):
    lower = rows & ((1 << local_bits) - 1)
    mine = plus_minus(odd_bits((rows >> local_bits) & position, 7))
    within = lower & (LANES - 1)
    sublane = lax.broadcasted_iota(jnp.int32, (8, LANES), 0)
    table = [plus_minus(odd_bits(sublane & within, 3)) * mine]
    for bit in range(3, 7):
        flip = plus_minus((within >> bit) & 1)
        table = table + [t * flip for t in table]
    return jnp.concatenate(table, axis=0).astype(jnp.bfloat16), lower >> 7


def regroup(block):
    row = lax.broadcasted_iota(jnp.int32, block.shape, 0) >> 2
    lane = lax.broadcasted_iota(jnp.int32, block.shape, 1) >> 5
    shift = (lane - row) & 3
    out = block
    for s in range(1, 4):
        turned = pltpu.roll(block, 32 * s, 1)
        turned = jnp.concatenate([turned[4 * s:], turned[:4 * s]], axis=0)
        out = jnp.where(shift == s, turned, out)
    return out


def sample_kernel(local_bits, position_ref, panel_ref, sign_ref, sample_ref, out_ref, half_ref, pair_ref):
    columns = panel_ref.shape[0]
    tiles = panel_ref.shape[1] // LANES
    inner = 8
    outer = tiles // inner
    for a in range(outer):
        parts = []
        for b in range(inner):
            tile = a * inner + b
            sign = sign_ref[tile:tile + 1, :].astype(jnp.float32)
            parts.append(panel_ref[:, tile * LANES:(tile + 1) * LANES] * sign)
        for b, part in enumerate(butterflies(parts)):
            half_ref[a * inner + b] = part
    for b in range(inner):
        parts = butterflies([half_ref[a * inner + b] for a in range(outer)])
        for a, part in enumerate(parts):
            tile = a * inner + b
            high = part.astype(jnp.bfloat16)
            low = (part - high.astype(jnp.float32)).astype(jnp.bfloat16)
            pair_ref[tile * columns:(tile + 1) * columns, :LANES] = high
            pair_ref[tile * columns:(tile + 1) * columns, LANES:] = low

    position = position_ref[0]
    groups = FOLD // LANES
    step = 256

    def one_fold(t, carry):
        tables, homes = [], []
        for g in range(groups):
            rows = sample_ref[pl.ds(t * groups + g, 1), :]
            table, home = sampled_table(rows, position, local_bits)
            tables.append(table)
            homes.append(home)
        table = jnp.concatenate(tables, axis=1)
        home = jnp.concatenate(homes, axis=1)
        table = jnp.concatenate([table, table], axis=0)
        picked = jnp.zeros((columns, FOLD), jnp.float32)
        for start in range(0, tiles * columns, step):
            values = jnp.dot(pair_ref[start:start + step, :], table, preferred_element_type=jnp.float32)
            for i in range(step // columns):
                tile = start // columns + i
                picked = jnp.where(home == tile, values[i * columns:(i + 1) * columns], picked)
        for g in range(groups):
            start = pl.multiple_of((t * groups + g) * 16, 16)
            out_ref[pl.ds(start, 16), :] = regroup(picked[:, g * LANES:(g + 1) * LANES])
        return carry

    lax.fori_loop(0, sample_ref.shape[0] // groups, one_fold, 0)


def sum_kernel(scale, parts_ref, out_ref):
    total = parts_ref[0:8, :]
    for start in range(8, parts_ref.shape[0], 8):
        total = total + parts_ref[start:start + 8, :]
    total = (total[0:4] + total[4:8]) * scale
    for j in range(4):
        out_ref[4 * j:4 * j + 4, :] = total[:, 32 * j:32 * j + 32]


def body(matrix_panel, row_signs, sample_rows):
    columns, length = matrix_panel.shape
    devices = lax.axis_size("rows")
    samples = sample_rows.shape[0]
    tiles = length // LANES
    position = lax.axis_index("rows").astype(jnp.int32).reshape(1)
    vmem = pl.BlockSpec(memory_space=pltpu.VMEM)
    partial = pl.pallas_call(
        functools.partial(sample_kernel, length.bit_length() - 1),
        out_shape=jax.ShapeDtypeStruct((samples * columns // LANES, LANES), jnp.float32),
        in_specs=[pl.BlockSpec(memory_space=pltpu.SMEM), vmem, vmem, vmem],
        out_specs=vmem,
        scratch_shapes=[
            pltpu.VMEM((tiles, columns, LANES), jnp.float32),
            pltpu.VMEM((tiles * columns, 2 * LANES), jnp.bfloat16),
        ],
        compiler_params=pltpu.CompilerParams(vmem_limit_bytes=32 * 2**20),
    )(position, matrix_panel, row_signs.reshape(tiles, LANES), sample_rows.reshape(samples // LANES, LANES))
    parts = lax.all_to_all(partial.reshape(devices, 4, LANES), "rows", 0, 0, tiled=True)
    return pl.pallas_call(
        functools.partial(sum_kernel, 1.0 / math.sqrt(length * devices)),
        out_shape=jax.ShapeDtypeStruct((columns, samples // devices), jnp.float32),
        in_specs=[vmem],
        out_specs=vmem,
    )(parts.reshape(devices * 4, LANES))


def solution(mesh):
    in_specs = (P(None, "rows"), P("rows"), P())
    out_specs = P(None, "rows")
    return jax.shard_map(body, mesh=mesh, in_specs=in_specs, out_specs=out_specs, check_vma=False)
```

```python
import functools
import math

import jax
import jax.numpy as jnp
from jax import lax
from jax.experimental import pallas as pl
from jax.experimental.pallas import tpu as pltpu
from jax.sharding import PartitionSpec as P

LANES = 128
FOLD = 256


def butterflies(parts):
    parts = list(parts)
    half = 1
    while half < len(parts):
        for i in range(len(parts)):
            if not i & half:
                low, high = parts[i], parts[i + half]
                parts[i], parts[i + half] = low + high, low - high
        half *= 2
    return parts


def odd_bits(x, width):
    shift = 1
    while shift < width:
        shift *= 2
    while shift > 1:
        shift //= 2
        x = x ^ (x >> shift)
    return x & 1


def plus_minus(bit):
    return (1 - 2 * bit).astype(jnp.float32)


def sampled_table(rows, position, local_bits):
    lower = rows & ((1 << local_bits) - 1)
    mine = plus_minus(odd_bits((rows >> local_bits) & position, 7))
    within = lower & (LANES - 1)
    sublane = lax.broadcasted_iota(jnp.int32, (8, LANES), 0)
    table = [plus_minus(odd_bits(sublane & within, 3)) * mine]
    for bit in range(3, 7):
        flip = plus_minus((within >> bit) & 1)
        table = table + [t * flip for t in table]
    return jnp.concatenate(table, axis=0).astype(jnp.bfloat16), lower >> 7


def regroup(block):
    row = lax.broadcasted_iota(jnp.int32, block.shape, 0) >> 2
    lane = lax.broadcasted_iota(jnp.int32, block.shape, 1) >> 5
    shift = (lane - row) & 3
    out = block
    for s in range(1, 4):
        turned = pltpu.roll(block, 32 * s, 1)
        turned = jnp.concatenate([turned[4 * s:], turned[:4 * s]], axis=0)
        out = jnp.where(shift == s, turned, out)
    return out


def sample_kernel(local_bits, position_ref, panel_hbm, sign_hbm, sample_hbm, out_hbm, panel_ref, sign_ref, sample_ref, half_ref, pair_ref, table_ref, home_ref, out_ref, panel_sems, out_sems, sems):
    columns, length = panel_ref.shape
    tiles = length // LANES
    inner = 8
    outer = tiles // inner
    sample_copy = pltpu.make_async_copy(sample_hbm, sample_ref, sems.at[0])
    sample_copy.start()
    sign_copy = pltpu.make_async_copy(sign_hbm, sign_ref, sems.at[1])
    sign_copy.start()
    pieces = panel_sems.shape[0]
    width = length // pieces
    panel_copies = []
    for p in range(pieces):
        part = pl.ds(p * width, width)
        panel_copies.append(pltpu.make_async_copy(panel_hbm.at[:, part], panel_ref.at[:, part], panel_sems.at[p]))
        panel_copies[-1].start()

    position = position_ref[0]
    sample_copy.wait()
    for g in range(sample_ref.shape[0]):
        table, home = sampled_table(sample_ref[g:g + 1, :], position, local_bits)
        table_ref[:, g * LANES:(g + 1) * LANES] = table
        home_ref[g:g + 1, :] = home

    sign_copy.wait()
    for a in range(outer):
        if a % (outer // pieces) == 0:
            panel_copies[a // (outer // pieces)].wait()
        parts = []
        for b in range(inner):
            tile = a * inner + b
            sign = sign_ref[tile:tile + 1, :].astype(jnp.float32)
            parts.append(panel_ref[:, tile * LANES:(tile + 1) * LANES] * sign)
        for b, part in enumerate(butterflies(parts)):
            half_ref[a * inner + b] = part
    for b in range(inner):
        parts = butterflies([half_ref[a * inner + b] for a in range(outer)])
        for a, part in enumerate(parts):
            tile = a * inner + b
            high = part.astype(jnp.bfloat16)
            low = (part - high.astype(jnp.float32)).astype(jnp.bfloat16)
            pair_ref[tile * columns:(tile + 1) * columns, :LANES] = high
            pair_ref[tile * columns:(tile + 1) * columns, LANES:] = low

    groups = FOLD // LANES
    step = 256
    folds = sample_ref.shape[0] // groups
    out_pieces = out_sems.shape[0]
    out_rows = out_ref.shape[0] // out_pieces
    out_copies = []
    for t in range(folds):
        table = table_ref[:, t * FOLD:(t + 1) * FOLD]
        table = jnp.concatenate([table, table], axis=0)
        home = jnp.concatenate([home_ref[t * groups + g:t * groups + g + 1, :] for g in range(groups)], axis=1)
        picked = jnp.zeros((columns, FOLD), jnp.float32)
        for start in range(0, tiles * columns, step):
            values = jnp.dot(pair_ref[start:start + step, :], table, preferred_element_type=jnp.float32)
            for i in range(step // columns):
                tile = start // columns + i
                picked = jnp.where(home == tile, values[i * columns:(i + 1) * columns], picked)
        for g in range(groups):
            row = (t * groups + g) * 16
            out_ref[row:row + 16, :] = regroup(picked[:, g * LANES:(g + 1) * LANES])
        if (t + 1) % (folds // out_pieces) == 0:
            p = len(out_copies)
            part = pl.ds(p * out_rows, out_rows)
            out_copies.append(pltpu.make_async_copy(out_ref.at[part], out_hbm.at[part], out_sems.at[p]))
            out_copies[-1].start()
    for copy in out_copies:
        copy.wait()


def body(matrix_panel, row_signs, sample_rows):
    columns, length = matrix_panel.shape
    devices = lax.axis_size("rows")
    samples = sample_rows.shape[0]
    tiles = length // LANES
    position = lax.axis_index("rows").astype(jnp.int32).reshape(1)
    hbm = pl.BlockSpec(memory_space=pltpu.HBM)
    groups = samples // LANES
    partial = pl.pallas_call(
        functools.partial(sample_kernel, length.bit_length() - 1),
        out_shape=jax.ShapeDtypeStruct((samples * columns // LANES, LANES), jnp.float32),
        in_specs=[pl.BlockSpec(memory_space=pltpu.SMEM), hbm, hbm, hbm],
        out_specs=hbm,
        scratch_shapes=[
            pltpu.VMEM((columns, length), jnp.float32),
            pltpu.VMEM((tiles, LANES), jnp.int32),
            pltpu.VMEM((groups, LANES), jnp.int32),
            pltpu.VMEM((tiles, columns, LANES), jnp.float32),
            pltpu.VMEM((tiles * columns, 2 * LANES), jnp.bfloat16),
            pltpu.VMEM((LANES, samples), jnp.bfloat16),
            pltpu.VMEM((groups, LANES), jnp.int32),
            pltpu.VMEM((samples * columns // LANES, LANES), jnp.float32),
            pltpu.SemaphoreType.DMA((4,)),
            pltpu.SemaphoreType.DMA((8,)),
            pltpu.SemaphoreType.DMA((2,)),
        ],
        compiler_params=pltpu.CompilerParams(vmem_limit_bytes=62 * 2**20),
    )(position, matrix_panel, row_signs.reshape(tiles, LANES), sample_rows.reshape(groups, LANES))
    parts = lax.all_to_all(partial.reshape(devices, 4, LANES), "rows", 0, 0, tiled=True)
    total = jnp.sum(parts, axis=0) * (1.0 / math.sqrt(length * devices))
    return jnp.concatenate([total[:, 32 * j:32 * j + 32] for j in range(4)], axis=0)


def solution(mesh):
    in_specs = (P(None, "rows"), P("rows"), P())
    out_specs = P(None, "rows")
    return jax.shard_map(body, mesh=mesh, in_specs=in_specs, out_specs=out_specs, check_vma=False)
```

```python
import functools
import math

import jax
import jax.numpy as jnp
from jax import lax
from jax.experimental import pallas as pl
from jax.experimental.pallas import tpu as pltpu
from jax.sharding import PartitionSpec as P

LANES = 128
FOLD = 256


def butterflies(parts):
    parts = list(parts)
    half = 1
    while half < len(parts):
        for i in range(len(parts)):
            if not i & half:
                low, high = parts[i], parts[i + half]
                parts[i], parts[i + half] = low + high, low - high
        half *= 2
    return parts


def odd_bits(x, width):
    shift = 1
    while shift < width:
        shift *= 2
    while shift > 1:
        shift //= 2
        x = x ^ (x >> shift)
    return x & 1


def plus_minus(bit):
    return (1 - 2 * bit).astype(jnp.float32)


def sampled_table(rows, position, local_bits):
    lower = rows & ((1 << local_bits) - 1)
    mine = plus_minus(odd_bits((rows >> local_bits) & position, 7))
    within = lower & (LANES - 1)
    sublane = lax.broadcasted_iota(jnp.int32, (8, LANES), 0)
    table = [plus_minus(odd_bits(sublane & within, 3)) * mine]
    for bit in range(3, 7):
        flip = plus_minus((within >> bit) & 1)
        table = table + [t * flip for t in table]
    return jnp.concatenate(table, axis=0).astype(jnp.bfloat16), lower >> 7


def regroup(block):
    row = lax.broadcasted_iota(jnp.int32, block.shape, 0) >> 2
    lane = lax.broadcasted_iota(jnp.int32, block.shape, 1) >> 5
    shift = (lane - row) & 3
    out = block
    for s in range(1, 4):
        turned = pltpu.roll(block, 32 * s, 1)
        turned = jnp.concatenate([turned[4 * s:], turned[:4 * s]], axis=0)
        out = jnp.where(shift == s, turned, out)
    return out


def choose(blocks, masks):
    for mask in masks:
        blocks = [jnp.where(mask, high, low) for low, high in zip(blocks[::2], blocks[1::2])]
    return blocks[0]


def sample_kernel(local_bits, position_ref, panel_ref, sign_ref, sample_ref, out_ref, half_ref, pair_ref):
    columns, length = panel_ref.shape
    tiles = length // LANES
    inner = 8
    outer = tiles // inner
    position = position_ref[0]
    for a in range(outer):
        parts = []
        for b in range(inner):
            tile = a * inner + b
            sign = sign_ref[tile:tile + 1, :].astype(jnp.float32)
            parts.append(panel_ref[:, tile * LANES:(tile + 1) * LANES] * sign)
        for b, part in enumerate(butterflies(parts)):
            half_ref[b * outer + a] = part
    for b in range(inner):
        parts = butterflies([half_ref[b * outer + a] for a in range(outer)])
        for a, part in enumerate(parts):
            row = (b * outer + a) * columns
            high = part.astype(jnp.bfloat16)
            low = (part - high.astype(jnp.float32)).astype(jnp.bfloat16)
            pair_ref[row:row + columns, :LANES] = high
            pair_ref[row:row + columns, LANES:] = low

    groups = FOLD // LANES
    step = outer * columns
    for t in range(sample_ref.shape[0] // groups):
        tables, masks = [], []
        for g in range(groups):
            row = t * groups + g
            table, home = sampled_table(sample_ref[row:row + 1, :], position, local_bits)
            tables.append(table)
            home = jnp.broadcast_to(home, (8, LANES))
            masks.append([(home & (1 << bit)) != 0 for bit in range(7)])
        table = jnp.concatenate(tables, axis=1)
        table = jnp.concatenate([table, table], axis=0)
        picked = {}
        for b in range(inner):
            values = jnp.dot(pair_ref[b * step:(b + 1) * step, :], table, preferred_element_type=jnp.float32)
            for g in range(groups):
                for h in range(0, columns, 8):
                    lanes = slice(g * LANES, (g + 1) * LANES)
                    blocks = [values[a * columns + h:a * columns + h + 8, lanes] for a in range(outer)]
                    picked[b, g, h] = choose(blocks, masks[g][3:])
        for g in range(groups):
            row = (t * groups + g) * columns
            chosen = [choose([picked[b, g, h] for b in range(inner)], masks[g][:3]) for h in range(0, columns, 8)]
            out_ref[row:row + columns, :] = regroup(jnp.concatenate(chosen, axis=0))


def body(matrix_panel, row_signs, sample_rows):
    columns, length = matrix_panel.shape
    devices = lax.axis_size("rows")
    samples = sample_rows.shape[0]
    tiles = length // LANES
    position = lax.axis_index("rows").astype(jnp.int32).reshape(1)
    vmem = pl.BlockSpec(memory_space=pltpu.VMEM)
    groups = samples // LANES
    partial = pl.pallas_call(
        functools.partial(sample_kernel, length.bit_length() - 1),
        out_shape=jax.ShapeDtypeStruct((samples * columns // LANES, LANES), jnp.float32),
        in_specs=[pl.BlockSpec(memory_space=pltpu.SMEM), vmem, vmem, vmem],
        out_specs=vmem,
        scratch_shapes=[
            pltpu.VMEM((tiles, columns, LANES), jnp.float32),
            pltpu.VMEM((tiles * columns, 2 * LANES), jnp.bfloat16),
        ],
        compiler_params=pltpu.CompilerParams(vmem_limit_bytes=32 * 2**20),
    )(position, -matrix_panel, row_signs.reshape(tiles, LANES), sample_rows.reshape(groups, LANES))
    parts = lax.all_to_all(partial.reshape(devices, 4, LANES), "rows", 0, 0, tiled=True)
    total = jnp.sum(parts, axis=0) * (-1.0 / math.sqrt(length * devices))
    return jnp.concatenate([total[:, 32 * j:32 * j + 32] for j in range(4)], axis=0)


def solution(mesh):
    in_specs = (P(None, "rows"), P("rows"), P())
    out_specs = P(None, "rows")
    return jax.shard_map(body, mesh=mesh, in_specs=in_specs, out_specs=out_specs, check_vma=False)
```

```python
import functools
import math

import jax
import jax.numpy as jnp
from jax import lax
from jax.experimental import pallas as pl
from jax.experimental.pallas import tpu as pltpu
from jax.sharding import PartitionSpec as P

LANES = 128
FOLD = 256
CHIP_ORDER = (2, 0, 3, 1)
FIRST_CHIP = 42


def butterflies(parts):
    parts = list(parts)
    half = 1
    while half < len(parts):
        for i in range(len(parts)):
            if not i & half:
                low, high = parts[i], parts[i + half]
                parts[i], parts[i + half] = low + high, low - high
        half *= 2
    return parts


def odd_bits(x, width):
    shift = 1
    while shift < width:
        shift *= 2
    while shift > 1:
        shift //= 2
        x = x ^ (x >> shift)
    return x & 1


def plus_minus(bit):
    return (1 - 2 * bit).astype(jnp.float32)


def sampled_table(rows, position, local_bits):
    lower = rows & ((1 << local_bits) - 1)
    mine = plus_minus(odd_bits((rows >> local_bits) & position, 7))
    within = lower & (LANES - 1)
    sublane = lax.broadcasted_iota(jnp.int32, (8, LANES), 0)
    table = [plus_minus(odd_bits(sublane & within, 3)) * mine]
    for bit in range(3, 7):
        flip = plus_minus((within >> bit) & 1)
        table = table + [t * flip for t in table]
    return jnp.concatenate(table, axis=0).astype(jnp.bfloat16), lower >> 7


def regroup(block):
    row = lax.broadcasted_iota(jnp.int32, block.shape, 0) >> 2
    lane = lax.broadcasted_iota(jnp.int32, block.shape, 1) >> 5
    shift = (lane - row) & 3
    out = block
    for s in range(1, 4):
        turned = pltpu.roll(block, 32 * s, 1)
        turned = jnp.concatenate([turned[4 * s:], turned[:4 * s]], axis=0)
        out = jnp.where(shift == s, turned, out)
    return out


def choose(blocks, masks):
    for mask in masks:
        blocks = [jnp.where(mask, high, low) for low, high in zip(blocks[::2], blocks[1::2])]
    return blocks[0]


def samples_of_core(sample_ref, core):
    samples = sample_ref[...]
    samples = jnp.where(core == 0, samples, pltpu.roll(samples, 96, 1))
    turned = pltpu.roll(samples, 32, 1)
    block = lax.broadcasted_iota(jnp.int32, (1, LANES), 1) >> 5
    return [
        jnp.where((block & 1) == 0, samples[2 * g + 1:2 * g + 2], turned[2 * g:2 * g + 1])
        for g in range(samples.shape[0] // 2)
    ]


def sample_folds(rows, position, local_bits, columns, pair_ref, out_ref):
    inner = 8
    outer = (1 << local_bits) // LANES // inner
    groups = FOLD // LANES
    step = outer * columns
    for t in range(len(rows) // groups):
        tables, masks = [], []
        for g in range(groups):
            table, home = sampled_table(rows[t * groups + g], position, local_bits)
            tables.append(table)
            home = jnp.broadcast_to(home, (8, LANES))
            masks.append([(home & (1 << bit)) != 0 for bit in range(7)])
        table = jnp.concatenate(tables, axis=1)
        table = jnp.concatenate([table, table], axis=0)
        picked = {}
        for b in range(inner):
            values = jnp.dot(pair_ref[b * step:(b + 1) * step, :], table, preferred_element_type=jnp.float32)
            for g in range(groups):
                for h in range(0, columns, 8):
                    lanes = slice(g * LANES, (g + 1) * LANES)
                    blocks = [values[a * columns + h:a * columns + h + 8, lanes] for a in range(outer)]
                    picked[b, g, h] = choose(blocks, masks[g][3:])
        for g in range(groups):
            row = ((t * groups + g) ^ (FIRST_CHIP // 4)) * columns
            chosen = [choose([picked[b, g, h] for b in range(inner)], masks[g][:3]) for h in range(0, columns, 8)]
            out_ref[row:row + columns, :] = regroup(jnp.concatenate(chosen, axis=0))


def partner_kernel(local_bits, position_ref, panel_ref, sign_ref, sample_ref, out_ref, pair_ref, half_ref):
    columns, length = panel_ref.shape
    tiles = length // LANES
    inner = 8
    outer = tiles // inner
    position = position_ref[0]
    for a in range(outer):
        parts = []
        for b in range(inner):
            tile = a * inner + b
            sign = sign_ref[tile:tile + 1, :].astype(jnp.float32)
            parts.append(panel_ref[:, tile * LANES:(tile + 1) * LANES] * sign)
        for b, part in enumerate(butterflies(parts)):
            half_ref[b * outer + a] = part
    for b in range(inner):
        parts = butterflies([half_ref[b * outer + a] for a in range(outer)])
        for a, part in enumerate(parts):
            row = (b * outer + a) * columns
            high = part.astype(jnp.bfloat16)
            low = (part - high.astype(jnp.float32)).astype(jnp.bfloat16)
            pair_ref[row:row + columns, :LANES] = high
            pair_ref[row:row + columns, LANES:] = low
    rows = samples_of_core(sample_ref, 1 - (position & 1))
    sample_folds(rows, position, local_bits, columns, pair_ref, out_ref)


def own_kernel(local_bits, columns, position_ref, pair_ref, sample_ref, out_ref):
    position = position_ref[0]
    rows = samples_of_core(sample_ref, position & 1)
    sample_folds(rows, position, local_bits, columns, pair_ref, out_ref)


def body(matrix_panel, row_signs, sample_rows):
    columns, length = matrix_panel.shape
    devices = lax.axis_size("rows")
    chips = devices // 2
    samples = sample_rows.shape[0]
    tiles = length // LANES
    local_bits = length.bit_length() - 1
    position = lax.axis_index("rows").astype(jnp.int32).reshape(1)
    sample_rows = sample_rows.reshape(samples // LANES, LANES)
    smem = pl.BlockSpec(memory_space=pltpu.SMEM)
    vmem = pl.BlockSpec(memory_space=pltpu.VMEM)
    params = pltpu.CompilerParams(vmem_limit_bytes=32 * 2**20)
    half_shape = jax.ShapeDtypeStruct((samples * columns // LANES // 2, LANES), jnp.float32)
    work = samples * columns * length
    partner, pair = pl.pallas_call(
        functools.partial(partner_kernel, local_bits),
        out_shape=(half_shape, jax.ShapeDtypeStruct((tiles * columns, 2 * LANES), jnp.bfloat16)),
        in_specs=[smem, vmem, vmem, vmem],
        out_specs=(vmem, vmem),
        scratch_shapes=[pltpu.VMEM((tiles, columns, LANES), jnp.float32)],
        compiler_params=params,
        cost_estimate=pl.CostEstimate(flops=2 * work, bytes_accessed=2**21, transcendentals=0),
    )(position, -matrix_panel, row_signs.reshape(tiles, LANES), sample_rows)
    arrived = lax.ppermute(partner.reshape(chips, 4, LANES), "rows", [(i, i ^ 1) for i in range(devices)])
    own = pl.pallas_call(
        functools.partial(own_kernel, local_bits, columns),
        out_shape=half_shape,
        in_specs=[smem, vmem, vmem],
        out_specs=vmem,
        compiler_params=params,
        cost_estimate=pl.CostEstimate(flops=2 * work, bytes_accessed=2**21, transcendentals=0),
    )(position, pair, sample_rows)
    partial = own.reshape(chips, 4, LANES) + arrived
    order = [4 * (p ^ (FIRST_CHIP // 4)) + chip for p in range(chips // 4) for chip in CHIP_ORDER]
    parts = lax.all_to_all(partial, "rows", 0, 0, axis_index_groups=[[2 * chip + core for chip in order] for core in range(2)], tiled=True)
    total = jnp.sum(parts, axis=0) * (-1.0 / math.sqrt(length * devices))
    return jnp.concatenate([total[:, 32 * j:32 * j + 32] for j in range(4)], axis=0)


def solution(mesh):
    in_specs = (P(None, "rows"), P("rows"), P())
    out_specs = P(None, "rows")
    return jax.shard_map(body, mesh=mesh, in_specs=in_specs, out_specs=out_specs, check_vma=False)
```

```python
import functools
import math

import jax
import jax.numpy as jnp
from jax import lax
from jax.experimental import pallas as pl
from jax.experimental.pallas import tpu as pltpu
from jax.sharding import PartitionSpec as P

LANES = 128
FOLD = 256
CHIP_ORDER = (2, 0, 3, 1)
FIRST_CHIP = 42
PARTNER_LOOKUPS = 14
OWN_LOOKUPS = 10


def butterflies(parts):
    parts = list(parts)
    half = 1
    while half < len(parts):
        for i in range(len(parts)):
            if not i & half:
                low, high = parts[i], parts[i + half]
                parts[i], parts[i + half] = low + high, low - high
        half *= 2
    return parts


def odd_bits(x, width):
    shift = 1
    while shift < width:
        shift *= 2
    while shift > 1:
        shift //= 2
        x = x ^ (x >> shift)
    return x & 1


def plus_minus(bit):
    return (1 - 2 * bit).astype(jnp.float32)


def sampled_table(rows, position, local_bits):
    within = rows & (LANES - 1)
    sublane = lax.broadcasted_iota(jnp.int32, (8, LANES), 0)
    table = [plus_minus(odd_bits(sublane & within, 3)) * sample_sign(rows, position, local_bits)]
    for bit in range(3, 7):
        flip = plus_minus((within >> bit) & 1)
        table = table + [t * flip for t in table]
    return jnp.concatenate(table, axis=0).astype(jnp.bfloat16)


def regroup(block):
    row = lax.broadcasted_iota(jnp.int32, block.shape, 0) >> 2
    lane = lax.broadcasted_iota(jnp.int32, block.shape, 1) >> 5
    shift = (lane - row) & 3
    out = block
    for s in range(1, 4):
        turned = pltpu.roll(block, 32 * s, 1)
        turned = jnp.concatenate([turned[4 * s:], turned[:4 * s]], axis=0)
        out = jnp.where(shift == s, turned, out)
    return out


def choose(blocks, masks):
    for mask in masks:
        blocks = [jnp.where(mask, high, low) for low, high in zip(blocks[::2], blocks[1::2])]
    return blocks[0]


def samples_of_core(sample_ref, core):
    samples = sample_ref[...]
    samples = jnp.where(core == 0, samples, pltpu.roll(samples, 96, 1))
    turned = pltpu.roll(samples, 32, 1)
    block = lax.broadcasted_iota(jnp.int32, (1, LANES), 1) >> 5
    return [
        jnp.where((block & 1) == 0, samples[2 * g + 1:2 * g + 2], turned[2 * g:2 * g + 1])
        for g in range(samples.shape[0] // 2)
    ]


def sample_sign(rows, position, local_bits):
    return plus_minus(odd_bits((rows >> local_bits) & position, 7))


def tile_masks(rows, local_bits):
    tile = jnp.broadcast_to((rows & ((1 << local_bits) - 1)) >> 7, (8, LANES))
    return [(tile & (1 << bit)) != 0 for bit in range(7)]


def store_group(group, chosen, out_ref):
    chosen = jnp.concatenate(chosen, axis=0)
    row = (group ^ (FIRST_CHIP // 4)) * chosen.shape[0]
    out_ref[row:row + chosen.shape[0], :] = regroup(chosen)


def matmul_fold(rows, first, position, local_bits, columns, pair_ref, out_ref):
    inner = 8
    outer = (1 << local_bits) // LANES // inner
    step = outer * columns
    table = jnp.concatenate([sampled_table(row, position, local_bits) for row in rows], axis=1)
    table = jnp.concatenate([table, table], axis=0)
    masks = [tile_masks(row, local_bits) for row in rows]
    picked = {}
    for b in range(inner):
        values = jnp.dot(pair_ref[b * step:(b + 1) * step, :], table, preferred_element_type=jnp.float32)
        for g in range(len(rows)):
            for h in range(0, columns, 8):
                lanes = slice(g * LANES, (g + 1) * LANES)
                blocks = [values[a * columns + h:a * columns + h + 8, lanes] for a in range(outer)]
                picked[b, g, h] = choose(blocks, masks[g][3:])
    for g in range(len(rows)):
        chosen = [choose([picked[b, g, h] for b in range(inner)], masks[g][:3]) for h in range(0, columns, 8)]
        store_group(first + g, chosen, out_ref)


def whole_table(columns, pair_ref, whole_ref):
    place = lax.broadcasted_iota(jnp.int32, (LANES, LANES), 0)
    lane = lax.broadcasted_iota(jnp.int32, (LANES, LANES), 1)
    signs = plus_minus(odd_bits(place & lane, 7)).astype(jnp.bfloat16)
    signs = jnp.concatenate([signs, signs], axis=1)
    step = 2 * LANES
    for b in range(pair_ref.shape[0] // step):
        part = lax.dot_general(
            signs, pair_ref[b * step:(b + 1) * step, :], (((1,), (1,)), ((), ())), preferred_element_type=jnp.float32
        )
        whole_ref[8 + b * step:8 + b * step + LANES, :] = part[:, :LANES]
        whole_ref[8 + b * step + LANES:8 + (b + 1) * step, :] = part[:, LANES:]


def whole_rows(rows, local_bits):
    lower = rows & ((1 << local_bits) - 1)
    tile = lower >> 7
    sublane = lax.broadcasted_iota(jnp.int32, rows.shape, 1) & 7
    return (((((tile & 7) << 1) | (tile >> 6)) << 7) | (lower & (LANES - 1))) + 8 - sublane


def lookup_group(row, group, slot, position, local_bits, columns, index_ref, whole_ref, out_ref):
    base = slot * LANES
    sublane = lax.broadcasted_iota(jnp.int32, (8, LANES), 0)
    blocks = []
    for k in range(0, LANES, 8):
        lines = whole_ref[pl.ds(index_ref[slot, k], 8), :]
        for j in range(1, 8):
            lines = jnp.where(sublane == j, whole_ref[pl.ds(index_ref[slot, k + j], 8), :], lines)
        blocks.append(lines)
    values = jnp.concatenate(blocks, axis=0).T
    masks = tile_masks(row, local_bits)[3:6]
    mine = jnp.broadcast_to(sample_sign(row, position, local_bits), (8, LANES))
    chosen = [
        choose([values[a * columns + h:a * columns + h + 8] for a in range(8)], masks) * mine
        for h in range(0, columns, 8)
    ]
    store_group(group, chosen, out_ref)


def matmul_all(rows, lookups, position, local_bits, columns, pair_ref, out_ref):
    for g in range(lookups, len(rows), 2):
        matmul_fold(rows[g:g + 2], g, position, local_bits, columns, pair_ref, out_ref)


def partner_kernel(local_bits, position_ref, panel_ref, sign_ref, sample_ref, out_ref, own_ref, pair_ref, half_ref, whole_ref, place_ref, index_ref, sem):
    columns, length = panel_ref.shape
    tiles = length // LANES
    inner = 8
    outer = tiles // inner
    position = position_ref[0]
    rows = samples_of_core(sample_ref, 1 - (position & 1))
    own_rows = samples_of_core(sample_ref, position & 1)
    lookups = [(row, g, out_ref) for g, row in enumerate(rows[:PARTNER_LOOKUPS])]
    lookups += [(row, g, own_ref) for g, row in enumerate(own_rows[:OWN_LOOKUPS])]
    for slot, (row, _, _) in enumerate(lookups):
        place_ref[slot:slot + 1, :] = whole_rows(row, local_bits)
    copy = pltpu.make_async_copy(place_ref, index_ref, sem)
    copy.start()
    for a in range(outer):
        parts = []
        for b in range(inner):
            tile = a * inner + b
            sign = sign_ref[tile:tile + 1, :].astype(jnp.float32)
            parts.append(panel_ref[:, tile * LANES:(tile + 1) * LANES] * sign)
        for b, part in enumerate(butterflies(parts)):
            half_ref[b * outer + a] = part
    for b in range(inner):
        parts = butterflies([half_ref[b * outer + a] for a in range(outer)])
        for a, part in enumerate(parts):
            row = (b * outer + a) * columns
            high = part.astype(jnp.bfloat16)
            low = (part - high.astype(jnp.float32)).astype(jnp.bfloat16)
            pair_ref[row:row + columns, :LANES] = high
            pair_ref[row:row + columns, LANES:] = low
    whole_table(columns, pair_ref, whole_ref)
    matmul_all(rows, PARTNER_LOOKUPS, position, local_bits, columns, pair_ref, out_ref)
    copy.wait()
    for slot, (row, group, target) in enumerate(lookups):
        lookup_group(row, group, slot, position, local_bits, columns, index_ref, whole_ref, target)


def own_kernel(local_bits, columns, position_ref, pair_ref, own_ref, sample_ref, out_ref):
    position = position_ref[0]
    rows = samples_of_core(sample_ref, position & 1)
    for g in range(OWN_LOOKUPS):
        start = (g ^ (FIRST_CHIP // 4)) * columns
        out_ref[start:start + columns, :] = own_ref[start:start + columns, :]
    matmul_all(rows, OWN_LOOKUPS, position, local_bits, columns, pair_ref, out_ref)


def body(matrix_panel, row_signs, sample_rows):
    columns, length = matrix_panel.shape
    devices = lax.axis_size("rows")
    chips = devices // 2
    samples = sample_rows.shape[0]
    tiles = length // LANES
    local_bits = length.bit_length() - 1
    position = lax.axis_index("rows").astype(jnp.int32).reshape(1)
    sample_rows = sample_rows.reshape(samples // LANES, LANES)
    smem = pl.BlockSpec(memory_space=pltpu.SMEM)
    vmem = pl.BlockSpec(memory_space=pltpu.VMEM)
    params = pltpu.CompilerParams(vmem_limit_bytes=32 * 2**20)
    half_shape = jax.ShapeDtypeStruct((samples * columns // LANES // 2, LANES), jnp.float32)
    work = samples * columns * length
    lookups = PARTNER_LOOKUPS + OWN_LOOKUPS
    partner, own, pair = pl.pallas_call(
        functools.partial(partner_kernel, local_bits),
        out_shape=(half_shape, half_shape, jax.ShapeDtypeStruct((tiles * columns, 2 * LANES), jnp.bfloat16)),
        in_specs=[smem, vmem, vmem, vmem],
        out_specs=(vmem, vmem, vmem),
        scratch_shapes=[
            pltpu.VMEM((tiles, columns, LANES), jnp.float32),
            pltpu.VMEM((tiles * columns + 16, LANES), jnp.float32),
            pltpu.VMEM((lookups, LANES), jnp.int32),
            pltpu.SMEM((lookups, LANES), jnp.int32),
            pltpu.SemaphoreType.DMA,
        ],
        compiler_params=params,
        cost_estimate=pl.CostEstimate(flops=2 * work, bytes_accessed=2**21, transcendentals=0),
    )(position, -matrix_panel, row_signs.reshape(tiles, LANES), sample_rows)
    arrived = lax.ppermute(partner.reshape(chips, 4, LANES), "rows", [(i, i ^ 1) for i in range(devices)])
    own = pl.pallas_call(
        functools.partial(own_kernel, local_bits, columns),
        out_shape=half_shape,
        in_specs=[smem, vmem, vmem, vmem],
        out_specs=vmem,
        compiler_params=params,
        cost_estimate=pl.CostEstimate(flops=2 * work, bytes_accessed=2**21, transcendentals=0),
    )(position, pair, own, sample_rows)
    partial = own.reshape(chips, 4, LANES) + arrived
    order = [4 * (p ^ (FIRST_CHIP // 4)) + chip for p in range(chips // 4) for chip in CHIP_ORDER]
    parts = lax.all_to_all(partial, "rows", 0, 0, axis_index_groups=[[2 * chip + core for chip in order] for core in range(2)], tiled=True)
    total = jnp.sum(parts, axis=0) * (-1.0 / math.sqrt(length * devices))
    return jnp.concatenate([total[:, 32 * j:32 * j + 32] for j in range(4)], axis=0)


def solution(mesh):
    in_specs = (P(None, "rows"), P("rows"), P())
    out_specs = P(None, "rows")
    return jax.shard_map(body, mesh=mesh, in_specs=in_specs, out_specs=out_specs, check_vma=False)
```

```python
import functools
import math

import jax
import jax.numpy as jnp
from jax import lax
from jax.experimental import pallas as pl
from jax.experimental.pallas import tpu as pltpu
from jax.sharding import PartitionSpec as P

LANES = 128
FOLD = 256
CHIP_ORDER = (2, 0, 3, 1)
FIRST_CHIP = 42
UNROLL = 4
PARTNER_LOOKUPS = 16
OWN_LOOKUPS = 10


def butterflies(parts):
    parts = list(parts)
    half = 1
    while half < len(parts):
        for i in range(len(parts)):
            if not i & half:
                low, high = parts[i], parts[i + half]
                parts[i], parts[i + half] = low + high, low - high
        half *= 2
    return parts


def odd_bits(x, width):
    shift = 1
    while shift < width:
        shift *= 2
    while shift > 1:
        shift //= 2
        x = x ^ (x >> shift)
    return x & 1


def plus_minus(bit):
    return (1 - 2 * bit).astype(jnp.float32)


def sampled_table(rows, position, local_bits):
    within = rows & (LANES - 1)
    sublane = lax.broadcasted_iota(jnp.int32, (8, LANES), 0)
    table = [plus_minus(odd_bits(sublane & within, 3)) * sample_sign(rows, position, local_bits)]
    for bit in range(3, 7):
        flip = plus_minus((within >> bit) & 1)
        table = table + [t * flip for t in table]
    return jnp.concatenate(table, axis=0).astype(jnp.bfloat16)


def regroup(block):
    row = lax.broadcasted_iota(jnp.int32, block.shape, 0) >> 2
    lane = lax.broadcasted_iota(jnp.int32, block.shape, 1) >> 5
    shift = (lane - row) & 3
    out = block
    for s in range(1, 4):
        turned = pltpu.roll(block, 32 * s, 1)
        turned = jnp.concatenate([turned[4 * s:], turned[:4 * s]], axis=0)
        out = jnp.where(shift == s, turned, out)
    return out


def choose(blocks, masks):
    for mask in masks:
        blocks = [jnp.where(mask, high, low) for low, high in zip(blocks[::2], blocks[1::2])]
    return blocks[0]


def samples_of_core(sample_ref, core):
    samples = sample_ref[...]
    samples = jnp.where(core == 0, samples, pltpu.roll(samples, 96, 1))
    turned = pltpu.roll(samples, 32, 1)
    block = lax.broadcasted_iota(jnp.int32, (1, LANES), 1) >> 5
    return [
        jnp.where((block & 1) == 0, samples[2 * g + 1:2 * g + 2], turned[2 * g:2 * g + 1])
        for g in range(samples.shape[0] // 2)
    ]


def sample_sign(rows, position, local_bits):
    return plus_minus(odd_bits((rows >> local_bits) & position, 7))


def tile_masks(rows, local_bits):
    tile = jnp.broadcast_to((rows & ((1 << local_bits) - 1)) >> 7, (8, LANES))
    return [(tile & (1 << bit)) != 0 for bit in range(7)]


def store_group(group, chosen, out_ref):
    chosen = jnp.concatenate(chosen, axis=0)
    row = (group ^ (FIRST_CHIP // 4)) * chosen.shape[0]
    out_ref[row:row + chosen.shape[0], :] = regroup(chosen)


def matmul_fold(rows, first, position, local_bits, columns, pair_ref, out_ref):
    inner = 8
    outer = (1 << local_bits) // LANES // inner
    step = outer * columns
    table = jnp.concatenate([sampled_table(row, position, local_bits) for row in rows], axis=1)
    table = jnp.concatenate([table, table], axis=0)
    masks = [tile_masks(row, local_bits) for row in rows]
    picked = {}
    for b in range(inner):
        values = jnp.dot(pair_ref[b * step:(b + 1) * step, :], table, preferred_element_type=jnp.float32)
        for g in range(len(rows)):
            for h in range(0, columns, 8):
                lanes = slice(g * LANES, (g + 1) * LANES)
                blocks = [values[a * columns + h:a * columns + h + 8, lanes] for a in range(outer)]
                picked[b, g, h] = choose(blocks, masks[g][3:])
    for g in range(len(rows)):
        chosen = [choose([picked[b, g, h] for b in range(inner)], masks[g][:3]) for h in range(0, columns, 8)]
        store_group(first + g, chosen, out_ref)


def whole_table(columns, pair_ref, whole_ref):
    place = lax.broadcasted_iota(jnp.int32, (LANES, LANES), 0)
    lane = lax.broadcasted_iota(jnp.int32, (LANES, LANES), 1)
    signs = plus_minus(odd_bits(place & lane, 7)).astype(jnp.bfloat16)
    signs = jnp.concatenate([signs, signs], axis=1)
    step = 2 * LANES
    for b in range(pair_ref.shape[0] // step):
        part = lax.dot_general(
            signs, pair_ref[b * step:(b + 1) * step, :], (((1,), (1,)), ((), ())), preferred_element_type=jnp.float32
        )
        whole_ref[8 + b * step:8 + b * step + LANES, :] = part[:, :LANES]
        whole_ref[8 + b * step + LANES:8 + (b + 1) * step, :] = part[:, LANES:]


def whole_rows(rows, local_bits):
    lower = rows & ((1 << local_bits) - 1)
    tile = lower >> 7
    sublane = lax.broadcasted_iota(jnp.int32, rows.shape, 1) & 7
    return (((((tile & 7) << 1) | (tile >> 6)) << 7) | (lower & (LANES - 1))) + 8 - sublane


def lookup_group(row, group, slot, position, local_bits, columns, index_ref, whole_ref, out_ref):
    base = slot * LANES
    sublane = lax.broadcasted_iota(jnp.int32, (8, LANES), 0)
    blocks = []
    for k in range(0, LANES, 8):
        lines = whole_ref[pl.ds(index_ref[slot, k], 8), :]
        for j in range(1, 8):
            lines = jnp.where(sublane == j, whole_ref[pl.ds(index_ref[slot, k + j], 8), :], lines)
        blocks.append(lines)
    values = jnp.concatenate(blocks, axis=0).T
    masks = tile_masks(row, local_bits)[3:6]
    mine = jnp.broadcast_to(sample_sign(row, position, local_bits), (8, LANES))
    chosen = [
        choose([values[a * columns + h:a * columns + h + 8] for a in range(8)], masks) * mine
        for h in range(0, columns, 8)
    ]
    store_group(group, chosen, out_ref)


def matmul_all(rows, lookups, position, local_bits, columns, pair_ref, out_ref):
    for g in range(lookups, len(rows), 2):
        matmul_fold(rows[g:g + 2], g, position, local_bits, columns, pair_ref, out_ref)


def partner_kernel(local_bits, position_ref, panel_ref, sign_ref, sample_ref, out_ref, own_ref, pair_ref, half_ref, whole_ref, place_ref, index_ref, sem):
    columns, length = panel_ref.shape
    tiles = length // LANES
    inner = 8
    outer = tiles // inner
    position = position_ref[0]
    rows = samples_of_core(sample_ref, 1 - (position & 1))
    own_rows = samples_of_core(sample_ref, position & 1)
    lookups = [(row, g, out_ref) for g, row in enumerate(rows[:PARTNER_LOOKUPS])]
    lookups += [(row, g, own_ref) for g, row in enumerate(own_rows[:OWN_LOOKUPS])]
    for slot, (row, _, _) in enumerate(lookups):
        place_ref[slot:slot + 1, :] = whole_rows(row, local_bits)
    copy = pltpu.make_async_copy(place_ref, index_ref, sem)
    copy.start()

    def first_half(a, carry):
        parts = []
        for b in range(inner):
            tile = a * inner + b
            sign = sign_ref[pl.ds(tile, 1), :].astype(jnp.float32)
            parts.append(panel_ref[:, pl.ds(pl.multiple_of(tile * LANES, LANES), LANES)] * sign)
        for b, part in enumerate(butterflies(parts)):
            half_ref[b * outer + a] = part
        return carry

    lax.fori_loop(0, outer, first_half, 0, unroll=UNROLL)
    for b in range(inner):
        parts = butterflies([half_ref[b * outer + a] for a in range(outer)])
        for a, part in enumerate(parts):
            row = (b * outer + a) * columns
            high = part.astype(jnp.bfloat16)
            low = (part - high.astype(jnp.float32)).astype(jnp.bfloat16)
            pair_ref[row:row + columns, :LANES] = high
            pair_ref[row:row + columns, LANES:] = low
    whole_table(columns, pair_ref, whole_ref)
    matmul_all(rows, PARTNER_LOOKUPS, position, local_bits, columns, pair_ref, out_ref)
    copy.wait()
    for slot, (row, group, target) in enumerate(lookups):
        lookup_group(row, group, slot, position, local_bits, columns, index_ref, whole_ref, target)


def own_kernel(local_bits, columns, position_ref, pair_ref, own_ref, sample_ref, out_ref):
    position = position_ref[0]
    rows = samples_of_core(sample_ref, position & 1)
    for g in range(OWN_LOOKUPS):
        start = (g ^ (FIRST_CHIP // 4)) * columns
        out_ref[start:start + columns, :] = own_ref[start:start + columns, :]
    matmul_all(rows, OWN_LOOKUPS, position, local_bits, columns, pair_ref, out_ref)


def sum_kernel(scale, parts_ref, out_ref):
    total = parts_ref[0:8, :]
    for start in range(8, parts_ref.shape[0], 8):
        total = total + parts_ref[start:start + 8, :]
    total = (total[0:4] + total[4:8]) * scale
    for j in range(4):
        out_ref[4 * j:4 * j + 4, :] = total[:, 32 * j:32 * j + 32]


def body(matrix_panel, row_signs, sample_rows):
    columns, length = matrix_panel.shape
    devices = lax.axis_size("rows")
    chips = devices // 2
    samples = sample_rows.shape[0]
    tiles = length // LANES
    local_bits = length.bit_length() - 1
    position = lax.axis_index("rows").astype(jnp.int32).reshape(1)
    sample_rows = sample_rows.reshape(samples // LANES, LANES)
    smem = pl.BlockSpec(memory_space=pltpu.SMEM)
    vmem = pl.BlockSpec(memory_space=pltpu.VMEM)
    params = pltpu.CompilerParams(vmem_limit_bytes=32 * 2**20)
    half_shape = jax.ShapeDtypeStruct((samples * columns // LANES // 2, LANES), jnp.float32)
    work = samples * columns * length
    lookups = PARTNER_LOOKUPS + OWN_LOOKUPS
    partner, own, pair = pl.pallas_call(
        functools.partial(partner_kernel, local_bits),
        out_shape=(half_shape, half_shape, jax.ShapeDtypeStruct((tiles * columns, 2 * LANES), jnp.bfloat16)),
        in_specs=[smem, vmem, vmem, vmem],
        out_specs=(vmem, vmem, vmem),
        scratch_shapes=[
            pltpu.VMEM((tiles, columns, LANES), jnp.float32),
            pltpu.VMEM((tiles * columns + 16, LANES), jnp.float32),
            pltpu.VMEM((lookups, LANES), jnp.int32),
            pltpu.SMEM((lookups, LANES), jnp.int32),
            pltpu.SemaphoreType.DMA,
        ],
        compiler_params=params,
        cost_estimate=pl.CostEstimate(flops=2 * work, bytes_accessed=2**21, transcendentals=0),
    )(position, -matrix_panel, row_signs.reshape(tiles, LANES), sample_rows)
    arrived = lax.ppermute(partner.reshape(chips, 4, LANES), "rows", [(i, i ^ 1) for i in range(devices)])
    own = pl.pallas_call(
        functools.partial(own_kernel, local_bits, columns),
        out_shape=half_shape,
        in_specs=[smem, vmem, vmem, vmem],
        out_specs=vmem,
        compiler_params=params,
        cost_estimate=pl.CostEstimate(flops=2 * work, bytes_accessed=2**21, transcendentals=0),
    )(position, pair, own, sample_rows)
    partial = own.reshape(chips, 4, LANES) + arrived
    order = [4 * (p ^ (FIRST_CHIP // 4)) + chip for p in range(chips // 4) for chip in CHIP_ORDER]
    parts = lax.all_to_all(partial, "rows", 0, 0, axis_index_groups=[[2 * chip + core for chip in order] for core in range(2)], tiled=True)
    return pl.pallas_call(
        functools.partial(sum_kernel, -1.0 / math.sqrt(length * devices)),
        out_shape=jax.ShapeDtypeStruct((columns, samples // devices), jnp.float32),
        in_specs=[vmem],
        out_specs=vmem,
        compiler_params=params,
    )(parts.reshape(chips * 4, LANES))


def solution(mesh):
    in_specs = (P(None, "rows"), P("rows"), P())
    out_specs = P(None, "rows")
    return jax.shard_map(body, mesh=mesh, in_specs=in_specs, out_specs=out_specs, check_vma=False)
```

```python
import functools
import math

import jax
import jax.numpy as jnp
from jax import lax
from jax.experimental import pallas as pl
from jax.experimental.pallas import tpu as pltpu
from jax.sharding import PartitionSpec as P

LANES = 128
FOLD = 256
CHIP_ORDER = (2, 0, 3, 1)
FIRST_CHIP = 58
UNROLL = 4
PARTNER_LOOKUPS = 16
OWN_LOOKUPS = 10
SHARED = 6


def butterflies(parts):
    parts = list(parts)
    half = 1
    while half < len(parts):
        for i in range(len(parts)):
            if not i & half:
                low, high = parts[i], parts[i + half]
                parts[i], parts[i + half] = low + high, low - high
        half *= 2
    return parts


def odd_bits(x, width):
    shift = 1
    while shift < width:
        shift *= 2
    while shift > 1:
        shift //= 2
        x = x ^ (x >> shift)
    return x & 1


def plus_minus(bit):
    return (1 - 2 * bit).astype(jnp.float32)


def sampled_table(rows, position, local_bits):
    within = rows & (LANES - 1)
    sublane = lax.broadcasted_iota(jnp.int32, (8, LANES), 0)
    table = [plus_minus(odd_bits(sublane & within, 3)) * sample_sign(rows, position, local_bits)]
    for bit in range(3, 7):
        flip = plus_minus((within >> bit) & 1)
        table = table + [t * flip for t in table]
    return jnp.concatenate(table, axis=0).astype(jnp.bfloat16)


def regroup(block):
    row = lax.broadcasted_iota(jnp.int32, block.shape, 0) >> 2
    lane = lax.broadcasted_iota(jnp.int32, block.shape, 1) >> 5
    shift = (lane - row) & 3
    out = block
    for s in range(1, 4):
        turned = pltpu.roll(block, 32 * s, 1)
        turned = jnp.concatenate([turned[4 * s:], turned[:4 * s]], axis=0)
        out = jnp.where(shift == s, turned, out)
    return out


def choose(blocks, masks):
    for mask in masks:
        blocks = [jnp.where(mask, high, low) for low, high in zip(blocks[::2], blocks[1::2])]
    return blocks[0]


def samples_of_core(sample_ref, core):
    samples = sample_ref[...]
    samples = jnp.where(core == 0, samples, pltpu.roll(samples, 96, 1))
    turned = pltpu.roll(samples, 32, 1)
    block = lax.broadcasted_iota(jnp.int32, (1, LANES), 1) >> 5
    return [
        jnp.where((block & 1) == 0, samples[2 * g + 1:2 * g + 2], turned[2 * g:2 * g + 1])
        for g in range(samples.shape[0] // 2)
    ]


def sample_sign(rows, position, local_bits):
    return plus_minus(odd_bits((rows >> local_bits) & position, 7))


def tile_masks(rows, local_bits):
    tile = jnp.broadcast_to((rows & ((1 << local_bits) - 1)) >> 7, (8, LANES))
    return [(tile & (1 << bit)) != 0 for bit in range(7)]


def store_group(group, chosen, out_ref):
    chosen = jnp.concatenate(chosen, axis=0)
    row = (group ^ (FIRST_CHIP // 4)) * chosen.shape[0]
    out_ref[row:row + chosen.shape[0], :] = regroup(chosen)


def matmul_fold(rows, first, position, local_bits, columns, pair_ref, out_ref):
    inner = 8
    outer = (1 << local_bits) // LANES // inner
    step = outer * columns
    table = jnp.concatenate([sampled_table(row, position, local_bits) for row in rows], axis=1)
    table = jnp.concatenate([table, table], axis=0)
    masks = [tile_masks(row, local_bits) for row in rows]
    picked = {}
    for b in range(inner):
        values = jnp.dot(pair_ref[b * step:(b + 1) * step, :], table, preferred_element_type=jnp.float32)
        for g in range(len(rows)):
            for h in range(0, columns, 8):
                lanes = slice(g * LANES, (g + 1) * LANES)
                blocks = [values[a * columns + h:a * columns + h + 8, lanes] for a in range(outer)]
                picked[b, g, h] = choose(blocks, masks[g][3:])
    for g in range(len(rows)):
        chosen = [choose([picked[b, g, h] for b in range(inner)], masks[g][:3]) for h in range(0, columns, 8)]
        store_group(first + g, chosen, out_ref)


def whole_table(columns, pair_ref, whole_ref):
    place = lax.broadcasted_iota(jnp.int32, (LANES, LANES), 0)
    lane = lax.broadcasted_iota(jnp.int32, (LANES, LANES), 1)
    signs = plus_minus(odd_bits(place & lane, 7)).astype(jnp.bfloat16)
    signs = jnp.concatenate([signs, signs], axis=1)
    step = 2 * LANES
    for b in range(pair_ref.shape[0] // step):
        part = lax.dot_general(
            signs, pair_ref[b * step:(b + 1) * step, :], (((1,), (1,)), ((), ())), preferred_element_type=jnp.float32
        )
        whole_ref[8 + b * step:8 + b * step + LANES, :] = part[:, :LANES]
        whole_ref[8 + b * step + LANES:8 + (b + 1) * step, :] = part[:, LANES:]


def whole_rows(rows, local_bits):
    lower = rows & ((1 << local_bits) - 1)
    tile = lower >> 7
    sublane = lax.broadcasted_iota(jnp.int32, rows.shape, 1) & 7
    return (((((tile & 7) << 1) | (tile >> 6)) << 7) | (lower & (LANES - 1))) + 8 - sublane


def lookup_group(row, group, slot, position, local_bits, columns, index_ref, whole_ref, out_ref):
    base = slot * LANES
    sublane = lax.broadcasted_iota(jnp.int32, (8, LANES), 0)
    blocks = []
    for k in range(0, LANES, 8):
        lines = whole_ref[pl.ds(index_ref[slot, k], 8), :]
        for j in range(1, 8):
            lines = jnp.where(sublane == j, whole_ref[pl.ds(index_ref[slot, k + j], 8), :], lines)
        blocks.append(lines)
    values = jnp.concatenate(blocks, axis=0).T
    masks = tile_masks(row, local_bits)[3:6]
    mine = jnp.broadcast_to(sample_sign(row, position, local_bits), (8, LANES))
    chosen = [
        choose([values[a * columns + h:a * columns + h + 8] for a in range(8)], masks) * mine
        for h in range(0, columns, 8)
    ]
    store_group(group, chosen, out_ref)


def matmul_all(rows, lookups, position, local_bits, columns, pair_ref, out_ref):
    for g in range(lookups, len(rows), 2):
        matmul_fold(rows[g:g + 2], g, position, local_bits, columns, pair_ref, out_ref)


def partner_kernel(local_bits, position_ref, panel_ref, sign_ref, sample_ref, out_ref, own_ref, pair_ref, whole_ref, half_ref, place_ref, index_ref, sem):
    columns, length = panel_ref.shape
    tiles = length // LANES
    inner = 8
    outer = tiles // inner
    position = position_ref[0]
    rows = samples_of_core(sample_ref, 1 - (position & 1))
    own_rows = samples_of_core(sample_ref, position & 1)
    lookups = [(row, g, out_ref) for g, row in enumerate(rows[:PARTNER_LOOKUPS])]
    lookups += [(row, g, own_ref) for g, row in enumerate(own_rows[:OWN_LOOKUPS])]
    for slot, (row, _, _) in enumerate(lookups):
        place_ref[slot:slot + 1, :] = whole_rows(row, local_bits)
    copy = pltpu.make_async_copy(place_ref, index_ref, sem)
    copy.start()

    def first_half(a, carry):
        parts = []
        for b in range(inner):
            tile = a * inner + b
            sign = sign_ref[pl.ds(tile, 1), :].astype(jnp.float32)
            parts.append(panel_ref[:, pl.ds(pl.multiple_of(tile * LANES, LANES), LANES)] * sign)
        for b, part in enumerate(butterflies(parts)):
            half_ref[b * outer + a] = part
        return carry

    lax.fori_loop(0, outer, first_half, 0, unroll=UNROLL)
    for b in range(inner):
        parts = butterflies([half_ref[b * outer + a] for a in range(outer)])
        for a, part in enumerate(parts):
            row = (b * outer + a) * columns
            high = part.astype(jnp.bfloat16)
            low = (part - high.astype(jnp.float32)).astype(jnp.bfloat16)
            pair_ref[row:row + columns, :LANES] = high
            pair_ref[row:row + columns, LANES:] = low
    whole_table(columns, pair_ref, whole_ref)
    matmul_all(rows, PARTNER_LOOKUPS, position, local_bits, columns, pair_ref, out_ref)
    copy.wait()
    for slot, (row, group, target) in enumerate(lookups[:PARTNER_LOOKUPS + SHARED]):
        lookup_group(row, group, slot, position, local_bits, columns, index_ref, whole_ref, target)

    @pl.when((position & 1) == 1)
    def _():
        for slot, (row, group, target) in enumerate(lookups):
            if slot >= PARTNER_LOOKUPS + SHARED:
                lookup_group(row, group, slot, position, local_bits, columns, index_ref, whole_ref, target)


def own_kernel(local_bits, columns, position_ref, pair_ref, whole_ref, own_ref, sample_ref, out_ref, place_ref, index_ref, sem):
    position = position_ref[0]
    rows = samples_of_core(sample_ref, position & 1)
    for g in range(SHARED, OWN_LOOKUPS):
        place_ref[g - SHARED:g - SHARED + 1, :] = whole_rows(rows[g], local_bits)
    copy = pltpu.make_async_copy(place_ref, index_ref, sem)
    copy.start()

    @pl.when(position >= 0)
    def _():
        for g in range(SHARED):
            start = (g ^ (FIRST_CHIP // 4)) * columns
            out_ref[start:start + columns, :] = own_ref[start:start + columns, :]
        matmul_all(rows, OWN_LOOKUPS, position, local_bits, columns, pair_ref, out_ref)

    copy.wait()

    @pl.when((position & 1) == 1)
    def _():
        for g in range(SHARED, OWN_LOOKUPS):
            start = (g ^ (FIRST_CHIP // 4)) * columns
            out_ref[start:start + columns, :] = own_ref[start:start + columns, :]

    @pl.when((position & 1) == 0)
    def _():
        for g in range(SHARED, OWN_LOOKUPS):
            lookup_group(rows[g], g, g - SHARED, position, local_bits, columns, index_ref, whole_ref, out_ref)


def sum_kernel(scale, parts_ref, out_ref):
    total = parts_ref[0:8, :]
    for start in range(8, parts_ref.shape[0], 8):
        total = total + parts_ref[start:start + 8, :]
    total = (total[0:4] + total[4:8]) * scale
    for j in range(4):
        out_ref[4 * j:4 * j + 4, :] = total[:, 32 * j:32 * j + 32]


def body(matrix_panel, row_signs, sample_rows):
    columns, length = matrix_panel.shape
    devices = lax.axis_size("rows")
    chips = devices // 2
    samples = sample_rows.shape[0]
    tiles = length // LANES
    local_bits = length.bit_length() - 1
    position = lax.axis_index("rows").astype(jnp.int32).reshape(1)
    sample_rows = sample_rows.reshape(samples // LANES, LANES)
    smem = pl.BlockSpec(memory_space=pltpu.SMEM)
    vmem = pl.BlockSpec(memory_space=pltpu.VMEM)
    params = pltpu.CompilerParams(vmem_limit_bytes=32 * 2**20)
    half_shape = jax.ShapeDtypeStruct((samples * columns // LANES // 2, LANES), jnp.float32)
    work = samples * columns * length
    lookups = PARTNER_LOOKUPS + OWN_LOOKUPS
    partner, own, pair, whole = pl.pallas_call(
        functools.partial(partner_kernel, local_bits),
        out_shape=(
            half_shape,
            half_shape,
            jax.ShapeDtypeStruct((tiles * columns, 2 * LANES), jnp.bfloat16),
            jax.ShapeDtypeStruct((tiles * columns + 16, LANES), jnp.float32),
        ),
        in_specs=[smem, vmem, vmem, vmem],
        out_specs=(vmem, vmem, vmem, vmem),
        scratch_shapes=[
            pltpu.VMEM((tiles, columns, LANES), jnp.float32),
            pltpu.VMEM((lookups, LANES), jnp.int32),
            pltpu.SMEM((lookups, LANES), jnp.int32),
            pltpu.SemaphoreType.DMA,
        ],
        compiler_params=params,
        cost_estimate=pl.CostEstimate(flops=2 * work, bytes_accessed=2**21, transcendentals=0),
    )(position, -matrix_panel, row_signs.reshape(tiles, LANES), sample_rows)
    arrived = lax.ppermute(partner.reshape(chips, 4, LANES), "rows", [(i, i ^ 1) for i in range(devices)])
    own = pl.pallas_call(
        functools.partial(own_kernel, local_bits, columns),
        out_shape=half_shape,
        in_specs=[smem, vmem, vmem, vmem, vmem],
        out_specs=vmem,
        scratch_shapes=[
            pltpu.VMEM((OWN_LOOKUPS - SHARED, LANES), jnp.int32),
            pltpu.SMEM((OWN_LOOKUPS - SHARED, LANES), jnp.int32),
            pltpu.SemaphoreType.DMA,
        ],
        compiler_params=params,
        cost_estimate=pl.CostEstimate(flops=2 * work, bytes_accessed=2**21, transcendentals=0),
    )(position, pair, whole, own, sample_rows)
    partial = own.reshape(chips, 4, LANES) + arrived
    order = [4 * (p ^ (FIRST_CHIP // 4)) + chip for p in range(chips // 4) for chip in CHIP_ORDER]
    parts = lax.all_to_all(partial, "rows", 0, 0, axis_index_groups=[[2 * chip + core for chip in order] for core in range(2)], tiled=True)
    return pl.pallas_call(
        functools.partial(sum_kernel, -1.0 / math.sqrt(length * devices)),
        out_shape=jax.ShapeDtypeStruct((columns, samples // devices), jnp.float32),
        in_specs=[vmem],
        out_specs=vmem,
        compiler_params=params,
    )(parts.reshape(chips * 4, LANES))


def solution(mesh):
    in_specs = (P(None, "rows"), P("rows"), P())
    out_specs = P(None, "rows")
    return jax.shard_map(body, mesh=mesh, in_specs=in_specs, out_specs=out_specs, check_vma=False)
```

```python
import functools
import math

import jax
import jax.numpy as jnp
from jax import lax
from jax.experimental import pallas as pl
from jax.experimental.pallas import tpu as pltpu
from jax.sharding import PartitionSpec as P

LANES = 128
FOLD = 256
CHIP_ORDER = (2, 0, 3, 1)
FIRST_CHIP = 58
UNROLL = 4
PARTNER_LOOKUPS = 16
OWN_LOOKUPS = 12
SHARED = 6


def butterflies(parts):
    parts = list(parts)
    half = 1
    while half < len(parts):
        for i in range(len(parts)):
            if not i & half:
                low, high = parts[i], parts[i + half]
                parts[i], parts[i + half] = low + high, low - high
        half *= 2
    return parts


def odd_bits(x, width):
    shift = 1
    while shift < width:
        shift *= 2
    while shift > 1:
        shift //= 2
        x = x ^ (x >> shift)
    return x & 1


def plus_minus(bit):
    return (1 - 2 * bit).astype(jnp.float32)


def sampled_table(rows, position, local_bits):
    within = rows & (LANES - 1)
    sublane = lax.broadcasted_iota(jnp.int32, (8, LANES), 0)
    table = [plus_minus(odd_bits(sublane & within, 3)) * sample_sign(rows, position, local_bits)]
    for bit in range(3, 7):
        flip = plus_minus((within >> bit) & 1)
        table = table + [t * flip for t in table]
    return jnp.concatenate(table, axis=0).astype(jnp.bfloat16)


def regroup(block):
    row = lax.broadcasted_iota(jnp.int32, block.shape, 0) >> 2
    lane = lax.broadcasted_iota(jnp.int32, block.shape, 1) >> 5
    shift = (lane - row) & 3
    out = block
    for s in range(1, 4):
        turned = pltpu.roll(block, 32 * s, 1)
        turned = jnp.concatenate([turned[4 * s:], turned[:4 * s]], axis=0)
        out = jnp.where(shift == s, turned, out)
    return out


def choose(blocks, masks):
    for mask in masks:
        blocks = [jnp.where(mask, high, low) for low, high in zip(blocks[::2], blocks[1::2])]
    return blocks[0]


def samples_of_core(sample_ref, core):
    samples = sample_ref[...]
    samples = jnp.where(core == 0, samples, pltpu.roll(samples, 96, 1))
    turned = pltpu.roll(samples, 32, 1)
    block = lax.broadcasted_iota(jnp.int32, (1, LANES), 1) >> 5
    return [
        jnp.where((block & 1) == 0, samples[2 * g + 1:2 * g + 2], turned[2 * g:2 * g + 1])
        for g in range(samples.shape[0] // 2)
    ]


def sample_sign(rows, position, local_bits):
    return plus_minus(odd_bits((rows >> local_bits) & position, 7))


def tile_masks(rows, local_bits):
    tile = jnp.broadcast_to((rows & ((1 << local_bits) - 1)) >> 7, (8, LANES))
    return [(tile & (1 << bit)) != 0 for bit in range(7)]


def store_group(group, chosen, out_ref):
    chosen = jnp.concatenate(chosen, axis=0)
    row = (group ^ (FIRST_CHIP // 4)) * chosen.shape[0]
    out_ref[row:row + chosen.shape[0], :] = regroup(chosen)


def matmul_fold(rows, first, position, local_bits, columns, pair_ref, out_ref):
    inner = 8
    outer = (1 << local_bits) // LANES // inner
    step = outer * columns
    table = jnp.concatenate([sampled_table(row, position, local_bits) for row in rows], axis=1)
    table = jnp.concatenate([table, table], axis=0)
    masks = [tile_masks(row, local_bits) for row in rows]
    picked = {}
    for b in range(inner):
        values = jnp.dot(pair_ref[b * step:(b + 1) * step, :], table, preferred_element_type=jnp.float32)
        for g in range(len(rows)):
            for h in range(0, columns, 8):
                lanes = slice(g * LANES, (g + 1) * LANES)
                blocks = [values[a * columns + h:a * columns + h + 8, lanes] for a in range(outer)]
                picked[b, g, h] = choose(blocks, masks[g][3:])
    for g in range(len(rows)):
        chosen = [choose([picked[b, g, h] for b in range(inner)], masks[g][:3]) for h in range(0, columns, 8)]
        store_group(first + g, chosen, out_ref)


def whole_table(columns, pair_ref, whole_ref):
    place = lax.broadcasted_iota(jnp.int32, (LANES, LANES), 0)
    lane = lax.broadcasted_iota(jnp.int32, (LANES, LANES), 1)
    signs = plus_minus(odd_bits(place & lane, 7)).astype(jnp.bfloat16)
    signs = jnp.concatenate([signs, signs], axis=1)
    step = 2 * LANES
    for b in range(pair_ref.shape[0] // step):
        part = lax.dot_general(
            signs, pair_ref[b * step:(b + 1) * step, :], (((1,), (1,)), ((), ())), preferred_element_type=jnp.float32
        )
        whole_ref[8 + b * step:8 + b * step + LANES, :] = part[:, :LANES]
        whole_ref[8 + b * step + LANES:8 + (b + 1) * step, :] = part[:, LANES:]


def whole_rows(rows, local_bits):
    lower = rows & ((1 << local_bits) - 1)
    tile = lower >> 7
    sublane = lax.broadcasted_iota(jnp.int32, rows.shape, 1) & 7
    return (((((tile & 7) << 1) | (tile >> 6)) << 7) | (lower & (LANES - 1))) + 8 - sublane


def lookup_group(row, group, slot, position, local_bits, columns, index_ref, whole_ref, out_ref):
    base = slot * LANES
    sublane = lax.broadcasted_iota(jnp.int32, (8, LANES), 0)
    blocks = []
    for k in range(0, LANES, 8):
        lines = whole_ref[pl.ds(index_ref[slot, k], 8), :]
        for j in range(1, 8):
            lines = jnp.where(sublane == j, whole_ref[pl.ds(index_ref[slot, k + j], 8), :], lines)
        blocks.append(lines)
    values = jnp.concatenate(blocks, axis=0).T
    masks = tile_masks(row, local_bits)[3:6]
    mine = jnp.broadcast_to(sample_sign(row, position, local_bits), (8, LANES))
    chosen = [
        choose([values[a * columns + h:a * columns + h + 8] for a in range(8)], masks) * mine
        for h in range(0, columns, 8)
    ]
    store_group(group, chosen, out_ref)


def matmul_all(rows, lookups, position, local_bits, columns, pair_ref, out_ref):
    for g in range(lookups, len(rows), 2):
        matmul_fold(rows[g:g + 2], g, position, local_bits, columns, pair_ref, out_ref)


def partner_kernel(local_bits, position_ref, panel_ref, sign_ref, sample_ref, out_ref, own_ref, pair_ref, whole_ref, half_ref, place_ref, index_ref, sem):
    columns, length = panel_ref.shape
    tiles = length // LANES
    inner = 8
    outer = tiles // inner
    position = position_ref[0]
    rows = samples_of_core(sample_ref, 1 - (position & 1))
    own_rows = samples_of_core(sample_ref, position & 1)
    lookups = [(row, g, out_ref) for g, row in enumerate(rows[:PARTNER_LOOKUPS])]
    lookups += [(row, g, own_ref) for g, row in enumerate(own_rows[:OWN_LOOKUPS])]
    for slot, (row, _, _) in enumerate(lookups):
        place_ref[slot:slot + 1, :] = whole_rows(row, local_bits)
    copy = pltpu.make_async_copy(place_ref, index_ref, sem)
    copy.start()

    def first_half(a, carry):
        parts = []
        for b in range(inner):
            tile = a * inner + b
            sign = sign_ref[pl.ds(tile, 1), :].astype(jnp.float32)
            parts.append(panel_ref[:, pl.ds(pl.multiple_of(tile * LANES, LANES), LANES)] * sign)
        for b, part in enumerate(butterflies(parts)):
            half_ref[b * outer + a] = part
        return carry

    lax.fori_loop(0, outer, first_half, 0, unroll=UNROLL)
    for b in range(inner):
        parts = butterflies([half_ref[b * outer + a] for a in range(outer)])
        for a, part in enumerate(parts):
            row = (b * outer + a) * columns
            high = part.astype(jnp.bfloat16)
            low = (part - high.astype(jnp.float32)).astype(jnp.bfloat16)
            pair_ref[row:row + columns, :LANES] = high
            pair_ref[row:row + columns, LANES:] = low
    whole_table(columns, pair_ref, whole_ref)
    matmul_all(rows, PARTNER_LOOKUPS, position, local_bits, columns, pair_ref, out_ref)
    copy.wait()
    for slot, (row, group, target) in enumerate(lookups[:PARTNER_LOOKUPS + SHARED]):
        lookup_group(row, group, slot, position, local_bits, columns, index_ref, whole_ref, target)

    @pl.when((position & 1) == 1)
    def _():
        for slot, (row, group, target) in enumerate(lookups):
            if slot >= PARTNER_LOOKUPS + SHARED:
                lookup_group(row, group, slot, position, local_bits, columns, index_ref, whole_ref, target)


def own_kernel(local_bits, columns, position_ref, pair_ref, whole_ref, own_ref, sample_ref, out_ref, place_ref, index_ref, sem):
    position = position_ref[0]
    rows = samples_of_core(sample_ref, position & 1)
    for g in range(SHARED, OWN_LOOKUPS):
        place_ref[g - SHARED:g - SHARED + 1, :] = whole_rows(rows[g], local_bits)
    copy = pltpu.make_async_copy(place_ref, index_ref, sem)
    copy.start()

    @pl.when(position >= 0)
    def _():
        for g in range(SHARED):
            start = (g ^ (FIRST_CHIP // 4)) * columns
            out_ref[start:start + columns, :] = own_ref[start:start + columns, :]
        matmul_all(rows, OWN_LOOKUPS, position, local_bits, columns, pair_ref, out_ref)

    copy.wait()

    @pl.when((position & 1) == 1)
    def _():
        for g in range(SHARED, OWN_LOOKUPS):
            start = (g ^ (FIRST_CHIP // 4)) * columns
            out_ref[start:start + columns, :] = own_ref[start:start + columns, :]

    @pl.when((position & 1) == 0)
    def _():
        for g in range(SHARED, OWN_LOOKUPS):
            lookup_group(rows[g], g, g - SHARED, position, local_bits, columns, index_ref, whole_ref, out_ref)


def sum_kernel(scale, parts_ref, out_ref):
    total = parts_ref[0:8, :]
    for start in range(8, parts_ref.shape[0], 8):
        total = total + parts_ref[start:start + 8, :]
    total = (total[0:4] + total[4:8]) * scale
    for j in range(4):
        out_ref[4 * j:4 * j + 4, :] = total[:, 32 * j:32 * j + 32]


def body(matrix_panel, row_signs, sample_rows):
    columns, length = matrix_panel.shape
    devices = lax.axis_size("rows")
    chips = devices // 2
    samples = sample_rows.shape[0]
    tiles = length // LANES
    local_bits = length.bit_length() - 1
    position = lax.axis_index("rows").astype(jnp.int32).reshape(1)
    sample_rows = sample_rows.reshape(samples // LANES, LANES)
    smem = pl.BlockSpec(memory_space=pltpu.SMEM)
    vmem = pl.BlockSpec(memory_space=pltpu.VMEM)
    params = pltpu.CompilerParams(vmem_limit_bytes=32 * 2**20)
    half_shape = jax.ShapeDtypeStruct((samples * columns // LANES // 2, LANES), jnp.float32)
    work = samples * columns * length
    lookups = PARTNER_LOOKUPS + OWN_LOOKUPS
    partner, own, pair, whole = pl.pallas_call(
        functools.partial(partner_kernel, local_bits),
        out_shape=(
            half_shape,
            half_shape,
            jax.ShapeDtypeStruct((tiles * columns, 2 * LANES), jnp.bfloat16),
            jax.ShapeDtypeStruct((tiles * columns + 16, LANES), jnp.float32),
        ),
        in_specs=[smem, vmem, vmem, vmem],
        out_specs=(vmem, vmem, vmem, vmem),
        scratch_shapes=[
            pltpu.VMEM((tiles, columns, LANES), jnp.float32),
            pltpu.VMEM((lookups, LANES), jnp.int32),
            pltpu.SMEM((lookups, LANES), jnp.int32),
            pltpu.SemaphoreType.DMA,
        ],
        compiler_params=params,
        cost_estimate=pl.CostEstimate(flops=2 * work, bytes_accessed=2**21, transcendentals=0),
    )(position, -matrix_panel, row_signs.reshape(tiles, LANES), sample_rows)
    arrived = lax.ppermute(partner.reshape(chips, 4, LANES), "rows", [(i, i ^ 1) for i in range(devices)])
    own = pl.pallas_call(
        functools.partial(own_kernel, local_bits, columns),
        out_shape=half_shape,
        in_specs=[smem, vmem, vmem, vmem, vmem],
        out_specs=vmem,
        scratch_shapes=[
            pltpu.VMEM((OWN_LOOKUPS - SHARED, LANES), jnp.int32),
            pltpu.SMEM((OWN_LOOKUPS - SHARED, LANES), jnp.int32),
            pltpu.SemaphoreType.DMA,
        ],
        compiler_params=params,
        cost_estimate=pl.CostEstimate(flops=2 * work, bytes_accessed=2**21, transcendentals=0),
    )(position, pair, whole, own, sample_rows)
    partial = own.reshape(chips, 4, LANES) + arrived
    order = [4 * (p ^ (FIRST_CHIP // 4)) + chip for p in range(chips // 4) for chip in CHIP_ORDER]
    parts = lax.all_to_all(partial, "rows", 0, 0, axis_index_groups=[[2 * chip + core for chip in order] for core in range(2)], tiled=True)
    return pl.pallas_call(
        functools.partial(sum_kernel, -1.0 / math.sqrt(length * devices)),
        out_shape=jax.ShapeDtypeStruct((columns, samples // devices), jnp.float32),
        in_specs=[vmem],
        out_specs=vmem,
        compiler_params=params,
    )(parts.reshape(chips * 4, LANES))


def solution(mesh):
    in_specs = (P(None, "rows"), P("rows"), P())
    out_specs = P(None, "rows")
    return jax.shard_map(body, mesh=mesh, in_specs=in_specs, out_specs=out_specs, check_vma=False)
```

```python
import functools
import math

import jax
import jax.numpy as jnp
from jax import lax
from jax.experimental import pallas as pl
from jax.experimental.pallas import tpu as pltpu
from jax.sharding import PartitionSpec as P

LANES = 128
FOLD = 256
CHIP_ORDER = (2, 0, 3, 1)
FIRST_CHIP = 58
UNROLL = 4
PARTNER_LOOKUPS = 16
OWN_LOOKUPS = 12
SHARED = 5


def butterflies(parts):
    parts = list(parts)
    half = 1
    while half < len(parts):
        for i in range(len(parts)):
            if not i & half:
                low, high = parts[i], parts[i + half]
                parts[i], parts[i + half] = low + high, low - high
        half *= 2
    return parts


def odd_bits(x, width):
    shift = 1
    while shift < width:
        shift *= 2
    while shift > 1:
        shift //= 2
        x = x ^ (x >> shift)
    return x & 1


def plus_minus(bit):
    return (1 - 2 * bit).astype(jnp.float32)


def sampled_table(rows, position, local_bits):
    within = rows & (LANES - 1)
    sublane = lax.broadcasted_iota(jnp.int32, (8, LANES), 0)
    table = [plus_minus(odd_bits(sublane & within, 3)) * sample_sign(rows, position, local_bits)]
    for bit in range(3, 7):
        flip = plus_minus((within >> bit) & 1)
        table = table + [t * flip for t in table]
    return jnp.concatenate(table, axis=0).astype(jnp.bfloat16)


def regroup(block):
    row = lax.broadcasted_iota(jnp.int32, block.shape, 0) >> 2
    lane = lax.broadcasted_iota(jnp.int32, block.shape, 1) >> 5
    shift = (lane - row) & 3
    out = block
    for s in range(1, 4):
        turned = pltpu.roll(block, 32 * s, 1)
        turned = jnp.concatenate([turned[4 * s:], turned[:4 * s]], axis=0)
        out = jnp.where(shift == s, turned, out)
    return out


def choose(blocks, masks):
    for mask in masks:
        blocks = [jnp.where(mask, high, low) for low, high in zip(blocks[::2], blocks[1::2])]
    return blocks[0]


def samples_of_core(sample_ref, core):
    samples = sample_ref[...]
    samples = jnp.where(core == 0, samples, pltpu.roll(samples, 96, 1))
    turned = pltpu.roll(samples, 32, 1)
    block = lax.broadcasted_iota(jnp.int32, (1, LANES), 1) >> 5
    return [
        jnp.where((block & 1) == 0, samples[2 * g + 1:2 * g + 2], turned[2 * g:2 * g + 1])
        for g in range(samples.shape[0] // 2)
    ]


def sample_sign(rows, position, local_bits):
    return plus_minus(odd_bits((rows >> local_bits) & position, 7))


def tile_masks(rows, local_bits):
    tile = jnp.broadcast_to((rows & ((1 << local_bits) - 1)) >> 7, (8, LANES))
    return [(tile & (1 << bit)) != 0 for bit in range(7)]


def store_group(group, chosen, out_ref):
    chosen = jnp.concatenate(chosen, axis=0)
    row = (group ^ (FIRST_CHIP // 4)) * chosen.shape[0]
    out_ref[row:row + chosen.shape[0], :] = regroup(chosen)


def matmul_fold(rows, first, position, local_bits, columns, pair_ref, out_ref):
    inner = 8
    outer = (1 << local_bits) // LANES // inner
    step = outer * columns
    table = jnp.concatenate([sampled_table(row, position, local_bits) for row in rows], axis=1)
    table = jnp.concatenate([table, table], axis=0)
    masks = [tile_masks(row, local_bits) for row in rows]
    picked = {}
    for b in range(inner):
        values = jnp.dot(pair_ref[b * step:(b + 1) * step, :], table, preferred_element_type=jnp.float32)
        for g in range(len(rows)):
            for h in range(0, columns, 8):
                lanes = slice(g * LANES, (g + 1) * LANES)
                blocks = [values[a * columns + h:a * columns + h + 8, lanes] for a in range(outer)]
                picked[b, g, h] = choose(blocks, masks[g][3:])
    for g in range(len(rows)):
        chosen = [choose([picked[b, g, h] for b in range(inner)], masks[g][:3]) for h in range(0, columns, 8)]
        store_group(first + g, chosen, out_ref)


def whole_table(columns, pair_ref, whole_ref):
    place = lax.broadcasted_iota(jnp.int32, (LANES, LANES), 0)
    lane = lax.broadcasted_iota(jnp.int32, (LANES, LANES), 1)
    signs = plus_minus(odd_bits(place & lane, 7)).astype(jnp.bfloat16)
    signs = jnp.concatenate([signs, signs], axis=1)
    step = 2 * LANES
    for b in range(pair_ref.shape[0] // step):
        part = lax.dot_general(
            signs, pair_ref[b * step:(b + 1) * step, :], (((1,), (1,)), ((), ())), preferred_element_type=jnp.float32
        )
        whole_ref[8 + b * step:8 + b * step + LANES, :] = part[:, :LANES]
        whole_ref[8 + b * step + LANES:8 + (b + 1) * step, :] = part[:, LANES:]


def whole_rows(rows, local_bits):
    lower = rows & ((1 << local_bits) - 1)
    tile = lower >> 7
    sublane = lax.broadcasted_iota(jnp.int32, rows.shape, 1) & 7
    return (((((tile & 7) << 1) | (tile >> 6)) << 7) | (lower & (LANES - 1))) + 8 - sublane


def lookup_group(row, group, slot, position, local_bits, columns, index_ref, whole_ref, out_ref):
    base = slot * LANES
    sublane = lax.broadcasted_iota(jnp.int32, (8, LANES), 0)
    blocks = []
    for k in range(0, LANES, 8):
        lines = whole_ref[pl.ds(index_ref[slot, k], 8), :]
        for j in range(1, 8):
            lines = jnp.where(sublane == j, whole_ref[pl.ds(index_ref[slot, k + j], 8), :], lines)
        blocks.append(lines)
    values = jnp.concatenate(blocks, axis=0).T
    masks = tile_masks(row, local_bits)[3:6]
    mine = jnp.broadcast_to(sample_sign(row, position, local_bits), (8, LANES))
    chosen = [
        choose([values[a * columns + h:a * columns + h + 8] for a in range(8)], masks) * mine
        for h in range(0, columns, 8)
    ]
    store_group(group, chosen, out_ref)


def matmul_all(rows, lookups, position, local_bits, columns, pair_ref, out_ref):
    for g in range(lookups, len(rows), 2):
        matmul_fold(rows[g:g + 2], g, position, local_bits, columns, pair_ref, out_ref)


def partner_kernel(local_bits, position_ref, panel_ref, sign_ref, sample_ref, out_ref, own_ref, pair_ref, whole_ref, half_ref, place_ref, index_ref, sem):
    columns, length = panel_ref.shape
    tiles = length // LANES
    inner = 8
    outer = tiles // inner
    position = position_ref[0]
    rows = samples_of_core(sample_ref, 1 - (position & 1))
    own_rows = samples_of_core(sample_ref, position & 1)
    lookups = [(row, g, out_ref) for g, row in enumerate(rows[:PARTNER_LOOKUPS])]
    lookups += [(row, g, own_ref) for g, row in enumerate(own_rows[:OWN_LOOKUPS])]
    for slot, (row, _, _) in enumerate(lookups):
        place_ref[slot:slot + 1, :] = whole_rows(row, local_bits)
    copy = pltpu.make_async_copy(place_ref, index_ref, sem)
    copy.start()

    def first_half(a, carry):
        parts = []
        for b in range(inner):
            tile = a * inner + b
            sign = sign_ref[pl.ds(tile, 1), :].astype(jnp.float32)
            parts.append(panel_ref[:, pl.ds(pl.multiple_of(tile * LANES, LANES), LANES)] * sign)
        for b, part in enumerate(butterflies(parts)):
            half_ref[b * outer + a] = part
        return carry

    lax.fori_loop(0, outer, first_half, 0, unroll=UNROLL)
    for b in range(inner):
        parts = butterflies([half_ref[b * outer + a] for a in range(outer)])
        for a, part in enumerate(parts):
            row = (b * outer + a) * columns
            high = part.astype(jnp.bfloat16)
            low = (part - high.astype(jnp.float32)).astype(jnp.bfloat16)
            pair_ref[row:row + columns, :LANES] = high
            pair_ref[row:row + columns, LANES:] = low
    whole_table(columns, pair_ref, whole_ref)
    matmul_all(rows, PARTNER_LOOKUPS, position, local_bits, columns, pair_ref, out_ref)
    copy.wait()
    for slot, (row, group, target) in enumerate(lookups[:PARTNER_LOOKUPS + SHARED]):
        lookup_group(row, group, slot, position, local_bits, columns, index_ref, whole_ref, target)

    @pl.when((position & 1) == 1)
    def _():
        for slot, (row, group, target) in enumerate(lookups):
            if slot >= PARTNER_LOOKUPS + SHARED:
                lookup_group(row, group, slot, position, local_bits, columns, index_ref, whole_ref, target)


def own_kernel(local_bits, columns, position_ref, pair_ref, whole_ref, own_ref, sample_ref, out_ref, place_ref, index_ref, sem):
    position = position_ref[0]
    rows = samples_of_core(sample_ref, position & 1)
    for g in range(SHARED, OWN_LOOKUPS):
        place_ref[g - SHARED:g - SHARED + 1, :] = whole_rows(rows[g], local_bits)
    copy = pltpu.make_async_copy(place_ref, index_ref, sem)
    copy.start()

    @pl.when(position >= 0)
    def _():
        for g in range(SHARED):
            start = (g ^ (FIRST_CHIP // 4)) * columns
            out_ref[start:start + columns, :] = own_ref[start:start + columns, :]
        matmul_all(rows, OWN_LOOKUPS, position, local_bits, columns, pair_ref, out_ref)

    copy.wait()

    @pl.when((position & 1) == 1)
    def _():
        for g in range(SHARED, OWN_LOOKUPS):
            start = (g ^ (FIRST_CHIP // 4)) * columns
            out_ref[start:start + columns, :] = own_ref[start:start + columns, :]

    @pl.when((position & 1) == 0)
    def _():
        for g in range(SHARED, OWN_LOOKUPS):
            lookup_group(rows[g], g, g - SHARED, position, local_bits, columns, index_ref, whole_ref, out_ref)


def sum_kernel(scale, parts_ref, out_ref):
    total = parts_ref[0:8, :]
    for start in range(8, parts_ref.shape[0], 8):
        total = total + parts_ref[start:start + 8, :]
    total = (total[0:4] + total[4:8]) * scale
    for j in range(4):
        out_ref[4 * j:4 * j + 4, :] = total[:, 32 * j:32 * j + 32]


def body(matrix_panel, row_signs, sample_rows):
    columns, length = matrix_panel.shape
    devices = lax.axis_size("rows")
    chips = devices // 2
    samples = sample_rows.shape[0]
    tiles = length // LANES
    local_bits = length.bit_length() - 1
    position = lax.axis_index("rows").astype(jnp.int32).reshape(1)
    sample_rows = sample_rows.reshape(samples // LANES, LANES)
    smem = pl.BlockSpec(memory_space=pltpu.SMEM)
    vmem = pl.BlockSpec(memory_space=pltpu.VMEM)
    params = pltpu.CompilerParams(vmem_limit_bytes=32 * 2**20)
    half_shape = jax.ShapeDtypeStruct((samples * columns // LANES // 2, LANES), jnp.float32)
    work = samples * columns * length
    lookups = PARTNER_LOOKUPS + OWN_LOOKUPS
    partner, own, pair, whole = pl.pallas_call(
        functools.partial(partner_kernel, local_bits),
        out_shape=(
            half_shape,
            half_shape,
            jax.ShapeDtypeStruct((tiles * columns, 2 * LANES), jnp.bfloat16),
            jax.ShapeDtypeStruct((tiles * columns + 16, LANES), jnp.float32),
        ),
        in_specs=[smem, vmem, vmem, vmem],
        out_specs=(vmem, vmem, vmem, vmem),
        scratch_shapes=[
            pltpu.VMEM((tiles, columns, LANES), jnp.float32),
            pltpu.VMEM((lookups, LANES), jnp.int32),
            pltpu.SMEM((lookups, LANES), jnp.int32),
            pltpu.SemaphoreType.DMA,
        ],
        compiler_params=params,
        cost_estimate=pl.CostEstimate(flops=2 * work, bytes_accessed=2**21, transcendentals=0),
    )(position, -matrix_panel, row_signs.reshape(tiles, LANES), sample_rows)
    arrived = lax.ppermute(partner.reshape(chips, 4, LANES), "rows", [(i, i ^ 1) for i in range(devices)])
    own = pl.pallas_call(
        functools.partial(own_kernel, local_bits, columns),
        out_shape=half_shape,
        in_specs=[smem, vmem, vmem, vmem, vmem],
        out_specs=vmem,
        scratch_shapes=[
            pltpu.VMEM((OWN_LOOKUPS - SHARED, LANES), jnp.int32),
            pltpu.SMEM((OWN_LOOKUPS - SHARED, LANES), jnp.int32),
            pltpu.SemaphoreType.DMA,
        ],
        compiler_params=params,
        cost_estimate=pl.CostEstimate(flops=2 * work, bytes_accessed=2**21, transcendentals=0),
    )(position, pair, whole, own, sample_rows)
    partial = own.reshape(chips, 4, LANES) + arrived
    order = [4 * (p ^ (FIRST_CHIP // 4)) + chip for p in range(chips // 4) for chip in CHIP_ORDER]
    parts = lax.all_to_all(partial, "rows", 0, 0, axis_index_groups=[[2 * chip + core for chip in order] for core in range(2)], tiled=True)
    return pl.pallas_call(
        functools.partial(sum_kernel, -1.0 / math.sqrt(length * devices)),
        out_shape=jax.ShapeDtypeStruct((columns, samples // devices), jnp.float32),
        in_specs=[vmem],
        out_specs=vmem,
        compiler_params=params,
    )(parts.reshape(chips * 4, LANES))


def solution(mesh):
    in_specs = (P(None, "rows"), P("rows"), P())
    out_specs = P(None, "rows")
    return jax.shard_map(body, mesh=mesh, in_specs=in_specs, out_specs=out_specs, check_vma=False)
```
